768 devices in a mesh: tp: 16 (over y, x_hi), fsdp: 48 (over x_lo, z, core).
Axes of the slice: x: 4 (x_hi: 2, x_lo: 2; x = x_hi * 2 + x_lo), y: 8, z: 12, core: 2. Of those that a mesh axis runs over, the one named last changes fastest.
Arguments:
- tokens: bfloat16 [512, 4608], P(None, 'tp'), may hold values from -6 to 6
- gate_weight: bfloat16 [4608, 36864], P('tp', 'fsdp'), may hold values from -0.09375 to 0.09375
- up_weight: bfloat16 [4608, 36864], P('tp', 'fsdp'), may hold values from -0.09375 to 0.09375
- down_weight: bfloat16 [36864, 4608], P('fsdp', 'tp'), may hold values from -0.03125 to 0.03125
- out_grad: bfloat16 [512, 4608], P(None, 'tp'), may hold values from -6 to 6
Outputs:
- mixed: bfloat16 [512, 4608], P(None, 'tp')
- tokens_grad: bfloat16 [512, 4608], P(None, 'tp')
- gate_grad: float32 [4608, 36864], P('tp', 'fsdp')
- up_grad: float32 [4608, 36864], P('tp', 'fsdp')
- down_grad: float32 [36864, 4608], P('fsdp', 'tp')
The draws below stay inside these ranges and needn't reach their ends.
All inputs are finite; a program needn't handle non-finite values.
Results may differ from the reference program's by a relative error of at most 0.005.
Values may be sent and summed in bfloat16 or wider, within the bound.
A program may use at most 32 MiB of HBM per device.

```python
import jax
import jax.numpy as jnp

D = 4608
FF = 36864
TOKENS = 512


def steps_of(own_key, shape, shards, low, top_value):
    gain, own = 1.0, jax.random.fold_in(own_key, 6)
    for axis_at, parts in shards:
        heights = jnp.exp(jax.random.uniform(jax.random.fold_in(own, axis_at), (parts,), jnp.float32, low / len(shards), top_value / len(shards)))
        gain = gain * jnp.repeat(heights, shape[axis_at] // parts).reshape([-1 if axis == axis_at else 1 for axis in range(len(shape))])
    return gain


def scatter_about(own_key, extent, scale, most, pieces=(), held_as=jnp.bfloat16):
    loudness = steps_of(own_key, extent, pieces, -0.22, 0.18) if pieces else 1.0
    drawn = jax.random.normal(own_key, extent, jnp.float32) * scale * loudness
    return jnp.minimum(jnp.maximum(drawn, -most), most).astype(held_as)


def setup_inputs(seed: int = 0) -> dict:
    key_of = jax.random.split(jax.random.key(seed), 6)
    tokens = scatter_about(key_of[0], (TOKENS, D), 1.0, 6.0, ((1, 16),))
    gate_weight = scatter_about(key_of[1], (D, FF), D ** -0.5, 0.09375, ((0, 16), (1, 48)))
    up_weight = scatter_about(key_of[2], (D, FF), D ** -0.5, 0.09375, ((0, 16), (1, 48)))
    down_weight = scatter_about(key_of[3], (FF, D), FF ** -0.5, 0.03125, ((0, 48), (1, 16)))
    out_grad = scatter_about(key_of[4], (TOKENS, D), 1.0, 6.0, ((1, 16),))
    return dict(tokens=tokens, gate_weight=gate_weight, up_weight=up_weight, down_weight=down_weight, out_grad=out_grad)


def reference(tokens, gate_weight, up_weight, down_weight, out_grad):
    gate = jnp.dot(tokens, gate_weight, preferred_element_type=jnp.float32)
    up = jnp.dot(tokens, up_weight, preferred_element_type=jnp.float32)
    hidden_back = jnp.dot(out_grad, down_weight.T, preferred_element_type=jnp.float32)
    sig = jax.nn.sigmoid(gate)
    activated = gate * sig
    hidden = (activated * up).astype(jnp.bfloat16)
    up_back = (hidden_back * activated).astype(jnp.bfloat16)
    gate_back = (hidden_back * up * sig * (1.0 + gate * (1.0 - sig))).astype(jnp.bfloat16)
    mixed = jnp.dot(hidden, down_weight, preferred_element_type=jnp.float32).astype(jnp.bfloat16)
    tokens_grad = jnp.dot(gate_back, gate_weight.T, preferred_element_type=jnp.float32)
    tokens_grad = (tokens_grad + jnp.dot(up_back, up_weight.T, preferred_element_type=jnp.float32)).astype(jnp.bfloat16)
    gate_grad = jnp.dot(tokens.T, gate_back, preferred_element_type=jnp.float32)
    up_grad = jnp.dot(tokens.T, up_back, preferred_element_type=jnp.float32)
    down_grad = jnp.dot(hidden.T, out_grad, preferred_element_type=jnp.float32)
    return (mixed, tokens_grad, gate_grad, up_grad, down_grad)
```

```python
import functools
import heapq

import jax
import jax.numpy as jnp
from jax import lax
from jax.experimental import pallas as pl
from jax.experimental.pallas import tpu as pltpu
from jax.sharding import PartitionSpec as P

MESH = pl.DeviceIdType.MESH
BF, F32 = jnp.bfloat16, jnp.float32
NY, NZ = 8, 12
TOKENS, DM, FF = 512, 288, 768
NC = 2
ROWS = TOKENS // NC
U = ROWS // 16
HALF = FF // 2
W3 = 3 * HALF
NSEM = 80 * NC


def contract(left, right, dims):
    return lax.dot_general(left, right, ((dims[:1], dims[1:]), ((), ())), preferred_element_type=F32)


def gating(sums):
    gate, up, back = sums[:, :HALF], sums[:, HALF : 2 * HALF], sums[:, 2 * HALF :]
    sig = jax.nn.sigmoid(gate)
    activated = gate * sig
    hidden = (activated * up).astype(BF)
    up_back = (back * activated).astype(BF)
    gate_back = (back * up * sig * (1.0 + gate * (1.0 - sig))).astype(BF)
    return hidden, gate_back, up_back


def kernel(
    tok, og, wg, wu, wd,
    mixed, tgrad, gg, ug, dg,
    part, sb1, rb1, sf1, rf1, tx, xr, sx, rx, sb2, rb2, sf2, rf2, gat1, gat2,
    wp, cr, av, xlr, bv, zr, fin, gbuf, ubuf, dbuf,
    ss, rs, ls,
):
    tp, fs = lax.axis_index("tp"), lax.axis_index("fsdp")
    y, xh = tp // 2, tp % 2
    xl, z, co = fs // 24, (fs // 2) % NZ, fs % 2

    def ymod(v):
        return lax.rem(v + 2 * NY, NY)

    def dev(dy=0, dxh=0, dxl=0, dz=0, dco=0):
        ny = ymod(y + dy)
        nxh = 1 - xh if dxh else xh
        nxl = 1 - xl if dxl else xl
        nz = lax.rem(z + dz, NZ)
        nco = 1 - co if dco else co
        return (ny * 2 + nxh, (nxl * NZ + nz) * 2 + nco)

    barrier = pltpu.get_barrier_semaphore()
    peers = [dev(dy=1), dev(dy=-1), dev(dxh=1), dev(dxl=1), dev(dco=1)]
    peers += [dev(dz=d) for d in range(1, NZ)]
    for peer in peers:
        pl.semaphore_signal(barrier, inc=1, device_id=peer, device_id_type=MESH)

    sent = []
    count = [0]

    def send(src, dst, to):
        i = count[0]
        count[0] += 1
        copy = pltpu.make_async_remote_copy(
            src_ref=src, dst_ref=dst, send_sem=ss.at[i], recv_sem=rs.at[i], device_id=to, device_id_type=MESH
        )
        copy.start()
        sent.append(copy)
        return copy

    ZORDER = [6, 5, 7, 4, 8, 3, 9, 2, 10, 1, 11]
    KORDER = [4, 3, -3, 2, -2, 1, -1, 0]

    def partial(st, c):
        rows = pl.ds(c * ROWS, ROWS)
        cols = pl.ds(st * HALF, HALF)
        for at, val in (
            (0, lambda: contract(tok[rows, :], wg[:, cols], (1, 0))),
            (1, lambda: contract(tok[rows, :], wu[:, cols], (1, 0))),
            (2, lambda: contract(og[rows, :], wd[cols, :], (1, 1))),
        ):
            part[st, c, :, :, :, at * HALF : (at + 1) * HALF] = val().reshape(NY, 2, U, HALF)

    def chain(value, long, sb, rb, sf, rf):
        got = {}
        todo = {}
        for sg, d in ((1, 0), (-1, 1)):
            first = 1 if sg == long else 2
            todo[sg] = (d, first)
        for s in range(1, 5):
            for sg in (1, -1):
                d, first = todo[sg]
                if s < first:
                    continue
                owner = ymod(y + sg * (5 - s))
                if s > first:
                    got[sg].wait_recv()
                val = value(owner, sg * (5 - s))
                if s > first:
                    val = val + rb[d, s - 2].astype(F32)
                if s == 4 and sg == long:
                    sf[...] = val
                    got[sg] = send(sf, rf, dev(dy=sg))
                else:
                    sb[d, s - 1] = val.astype(BF)
                    got[sg] = send(sb.at[d, s - 1], rb.at[d, s - 1], dev(dy=sg))
            yield
        for sg in (1, -1):
            got[sg].wait_recv()
        d = 1 if long == 1 else 0
        return value(y, 0) + rf[...] + rb[d, 3].astype(F32)

    def spread(slot, long, arrived):
        got = {}
        for s in range(1, 5):
            for sg in (1, -1):
                if s == 4 and sg != long:
                    continue
                if s > 1:
                    got[sg].wait_recv()
                    arrived(ymod(y - sg * (s - 1)))
                at = slot(ymod(y - sg * (s - 1)))
                got[sg] = send(at, at, dev(dy=sg))
            yield
        got[long].wait_recv()
        arrived(ymod(y - long * 4))
        got[-long].wait_recv()
        arrived(ymod(y + long * 3))

    def keep(at, sums):
        hidden, gate_back, up_back = gating(sums)
        at[:, :HALF] = hidden
        at[:, HALF : 2 * HALF] = gate_back
        at[:, 2 * HALF :] = up_back

    def stream0(c):
        long = 1 if c % 2 == 0 else -1

        def value(owner, _):
            return part[0, c, owner]

        total = yield from chain(value, long, sb1.at[c], rb1.at[c], sf1.at[c], rf1.at[c])
        tx[c] = total
        got = send(tx.at[c, 1 - xh], xr.at[c], dev(dxh=1))
        yield
        got.wait_recv()
        keep(gat1.at[c, y, xh], tx[c, xh] + xr[c])
        got = send(gat1.at[c, y, xh], gat1.at[c, y, xh], dev(dxh=1))
        yield
        got.wait_recv()
        yield from spread(lambda o: gat1.at[c, o], long, lambda o: None)

    def stream1_open(c):
        out = {}
        for k, off in enumerate(KORDER):
            sx[c, k] = part[1, c, ymod(y + off), 1 - xh].astype(BF)
            out[off] = send(sx.at[c, k], rx.at[c, k], dev(dxh=1))
        return out

    def stream1(c, from_x):
        long = -1 if c % 2 == 0 else 1
        ready = set()

        def value(owner, off):
            off = 4 if off == -4 else off
            if off not in ready:
                from_x[off].wait_recv()
                ready.add(off)
            k = KORDER.index(off)
            return part[1, c, owner, xh] + rx[c, k].astype(F32)

        yield
        total = yield from chain(value, long, sb2.at[c], rb2.at[c], sf2.at[c], rf2.at[c])
        keep(gat2.at[c, y, xh], total)
        back = []

        def arrived(o):
            back.append(send(gat2.at[c, o, xh], gat2.at[c, o, xh], dev(dxh=1)))

        arrived(y)
        yield from spread(lambda o: gat2.at[c, o, xh], long, arrived)
        yield
        for copy in back:
            copy.wait_recv()

    def reduce(c):
        one = gat1[c].reshape(ROWS, W3)
        two = gat2[c].reshape(ROWS, W3)

        def put(m, val):
            for h in range(2):
                rows = val[h * (ROWS // 2) : (h + 1) * (ROWS // 2)]
                wp[c, m, h, 0] = rows[:, :128]
                wp[c, m, h, 1] = rows[:, 128:256]
                wp[c, m, h, 2, :, :32] = rows[:, 256:]
                wp[c, m, h, 2, :, 32:] = jnp.zeros((ROWS // 2, 96), F32)

        put(0, contract(one[:, :HALF], wd[:HALF, :], (1, 0)) + contract(two[:, :HALF], wd[HALF:, :], (1, 0)))
        put(
            1,
            contract(one[:, HALF : 2 * HALF], wg[:, :HALF], (1, 1))
            + contract(two[:, HALF : 2 * HALF], wg[:, HALF:], (1, 1))
            + contract(one[:, 2 * HALF :], wu[:, :HALF], (1, 1))
            + contract(two[:, 2 * HALF :], wu[:, HALF:], (1, 1)),
        )
        got = send(wp.at[c, 1 - co], cr.at[c], dev(dco=1))
        yield
        got.wait_recv()
        av[c] = wp[c, co, 1 - xl] + cr[c, 1 - xl]
        got = send(av.at[c], xlr.at[c], dev(dxl=1))
        yield
        got.wait_recv()
        bv[c] = (wp[c, co, xl] + cr[c, xl] + xlr[c]).reshape(NZ, ROWS // 8, 128)
        gots = [send(bv.at[c, lax.rem(z + d, NZ)], zr.at[c, d - 1], dev(dz=d)) for d in ZORDER]
        yield
        for copy in gots:
            copy.wait_recv()
        total = bv[c, z]
        for d in range(NZ - 1):
            total = total + zr[c, d]
        fin[c, co, xl, z] = total.astype(BF)
        mine = fin.at[c, co, xl, z]
        gots = [send(mine, mine, dev(dz=d)) for d in ZORDER]
        yield
        for copy in gots:
            copy.wait_recv()
        mine = fin.at[c, co, xl]
        across = send(mine, mine, dev(dxl=1))
        near = send(mine, mine, dev(dco=1))
        yield
        across.wait_recv()
        mine = fin.at[c, co, 1 - xl]
        far = send(mine, mine, dev(dco=1))
        yield
        near.wait_recv()
        far.wait_recv()
        for m, out in ((0, mixed), (1, tgrad)):
            for h in range(2):
                rows = pl.ds(c * ROWS + h * (ROWS // 2), ROWS // 2)
                block = fin[c, m, h].reshape(3, ROWS // 2, 128)
                out[rows, 0:128] = block[0]
                out[rows, 128:256] = block[1]
                out[rows, 256:288] = block[2, :, :32]

    local = []

    def weight_grads():
        for st, g in ((0, gat1), (1, gat2)):
            cols = pl.ds(st * HALF, HALF)
            whole = g[...].reshape(TOKENS, W3)
            gbuf[:, cols] = contract(tok[...], whole[:, HALF : 2 * HALF], (0, 0))
            ubuf[:, cols] = contract(tok[...], whole[:, 2 * HALF :], (0, 0))
            dbuf[cols, :] = contract(whole[:, :HALF], og[...], (0, 0))
        for i, (a, b) in enumerate(((gbuf, gg), (ubuf, ug), (dbuf, dg))):
            copy = pltpu.make_async_copy(a, b, ls.at[i])
            copy.start()
            local.append(copy)

    partial(1, 0)
    pl.semaphore_wait(barrier, len(peers))
    opened = [stream1_open(0)]
    partial(0, 0)
    first = stream0(0)
    next(first)
    tasks = {("a", 0): first}
    for c in range(1, NC):
        partial(1, c)
        opened.append(stream1_open(c))
        partial(0, c)
        tasks["a", c] = stream0(c)
        next(tasks["a", c])
    for c in range(NC):
        tasks["b", c] = stream1(c, opened[c])
        next(tasks["b", c])

    def step(task):
        try:
            next(task)
            return True
        except StopIteration:
            return False

    def chunk(c):
        live = [tasks["a", c], tasks["b", c]]
        while live:
            live = [t for t in live if step(t)]
            yield
        yield from reduce(c)

    def last():
        while True:
            if state["gathered"] == NC:
                weight_grads()
                return
            yield

    live = [chunk(c) for c in range(NC)]
    rounds = 0
    done_grads = False
    while live:
        live = [t for t in live if step(t)]
        rounds += 1
        if rounds == GRADS_AT:
            weight_grads()
            done_grads = True
    if not done_grads:
        weight_grads()
    for copy in sent:
        copy.wait_send()
    for copy in local:
        copy.wait()


GRADS_AT = 99


def shards(tokens, gate_weight, up_weight, down_weight, out_grad):
    vm = pl.BlockSpec(memory_space=pltpu.VMEM)
    hbm = pl.BlockSpec(memory_space=pl.ANY)
    V = pltpu.VMEM
    q = ROWS // 2
    return pl.pallas_call(
        kernel,
        out_shape=(
            jax.ShapeDtypeStruct((TOKENS, DM), BF),
            jax.ShapeDtypeStruct((TOKENS, DM), BF),
            jax.ShapeDtypeStruct((DM, FF), F32),
            jax.ShapeDtypeStruct((DM, FF), F32),
            jax.ShapeDtypeStruct((FF, DM), F32),
        ),
        in_specs=[vm] * 5,
        out_specs=(vm, vm, hbm, hbm, hbm),
        scratch_shapes=[
            V((2, NC, NY, 2, U, W3), F32),
            V((NC, 2, 4, 2, U, W3), BF),
            V((NC, 2, 4, 2, U, W3), BF),
            V((NC, 2, U, W3), F32),
            V((NC, 2, U, W3), F32),
            V((NC, 2, U, W3), F32),
            V((NC, U, W3), F32),
            V((NC, NY, U, W3), BF),
            V((NC, NY, U, W3), BF),
            V((NC, 2, 4, U, W3), BF),
            V((NC, 2, 4, U, W3), BF),
            V((NC, U, W3), F32),
            V((NC, U, W3), F32),
            V((NC, NY, 2, U, W3), BF),
            V((NC, NY, 2, U, W3), BF),
            V((NC, 2, 2, 3, q, 128), F32),
            V((NC, 2, 3, q, 128), F32),
            V((NC, 3, q, 128), F32),
            V((NC, 3, q, 128), F32),
            V((NC, NZ, q // 4, 128), F32),
            V((NC, NZ - 1, q // 4, 128), F32),
            V((NC, 2, 2, NZ, q // 4, 128), BF),
            V((DM, FF), F32),
            V((DM, FF), F32),
            V((FF, DM), F32),
            pltpu.SemaphoreType.DMA((NSEM,)),
            pltpu.SemaphoreType.DMA((NSEM,)),
            pltpu.SemaphoreType.DMA((3,)),
        ],
        compiler_params=pltpu.CompilerParams(
            collective_id=0, has_side_effects=True, vmem_limit_bytes=56 << 20
        ),
        name="swiglu",
    )(tokens, out_grad, gate_weight, up_weight, down_weight)


def solution(mesh):
    placed = (P(None, "tp"), P("tp", "fsdp"), P("tp", "fsdp"), P("fsdp", "tp"), P(None, "tp"))
    return jax.shard_map(
        shards,
        mesh=mesh,
        in_specs=placed,
        out_specs=(P(None, "tp"), P(None, "tp"), P("tp", "fsdp"), P("tp", "fsdp"), P("fsdp", "tp")),
        check_vma=False,
    )
```

```python
import heapq

import jax
import jax.numpy as jnp
from jax import lax
from jax.experimental import pallas as pl
from jax.experimental.pallas import tpu as pltpu
from jax.sharding import PartitionSpec as P

MESH = pl.DeviceIdType.MESH
BF, F32 = jnp.bfloat16, jnp.float32
NY, NZ = 8, 12
TOKENS, DM, FF = 512, 288, 768
NC = 2
ROWS = TOKENS // NC
U = ROWS // 16
HALF = FF // 2
W3 = 3 * HALF
Q = ROWS // 2
NSEM = 45 * NC
LAG, T_Y, T_X, T_CORE, T_XL, T_Z = 1.5, 4.0, 4.5, 2.5, 3.6, 5.0
T_OPEN = (3.5, 5.0)


def contract(left, right, dims):
    return lax.dot_general(left, right, ((dims[:1], dims[1:]), ((), ())), preferred_element_type=F32)


def gating(sums):
    gate, up, back = sums[:, :HALF], sums[:, HALF : 2 * HALF], sums[:, 2 * HALF :]
    sig = jax.nn.sigmoid(gate)
    activated = gate * sig
    hidden = (activated * up).astype(BF)
    up_back = (back * activated).astype(BF)
    gate_back = (back * up * sig * (1.0 + gate * (1.0 - sig))).astype(BF)
    return hidden, gate_back, up_back


def kernel(
    tok_h, og_h, wg_h, wu_h, wd_h,
    mixed, tgrad, gg, ug, dg,
    part, sb1, rb1, sf1, rf1, tx, xr, sx, rx, sb2, rb2, sf2, rf2, gat1, gat2,
    wp, cr, av, xlr, bv, bs, zr, fin, gbuf, ubuf, dbuf, tok, og, tok_t, og_t, wg, wu, wd,
    ss, rs, ls, ins,
):
    tp, fs = lax.axis_index("tp"), lax.axis_index("fsdp")
    y, xh = tp // 2, tp % 2
    xl, z, co = fs // 24, (fs // 2) % NZ, fs % 2

    def ymod(v):
        return lax.rem(v + 2 * NY, NY)

    def dev(dy=0, dxh=0, dxl=0, dz=0, dco=0):
        ny = ymod(y + dy)
        nxh = 1 - xh if dxh else xh
        nxl = 1 - xl if dxl else xl
        nz = lax.rem(z + dz, NZ)
        nco = 1 - co if dco else co
        return (ny * 2 + nxh, (nxl * NZ + nz) * 2 + nco)

    barrier = pltpu.get_barrier_semaphore()
    peers = [dev(dy=1), dev(dy=-1), dev(dxh=1), dev(dxl=1), dev(dco=1)]
    peers += [dev(dz=d) for d in range(1, NZ)]
    for peer in peers:
        pl.semaphore_signal(barrier, inc=1, device_id=peer, device_id_type=MESH)

    loads = {}
    for i, (name, a, b) in enumerate(
        (("tok", tok_h, tok_t), ("wg", wg_h, wg), ("wu", wu_h, wu), ("og", og_h, og_t), ("wd", wd_h, wd))
    ):
        loads[name] = pltpu.make_async_copy(a, b, ins.at[i])
        loads[name].start()

    sent = []
    count = [0]

    def send(src, dst, to, at=None):
        i = count[0] if at is None else at
        count[0] += at is None
        copy = pltpu.make_async_remote_copy(
            src_ref=src, dst_ref=dst, send_sem=ss.at[i], recv_sem=rs.at[i], device_id=to, device_id_type=MESH
        )
        copy.start()
        if at is None:
            sent.append(copy)
        return copy

    def group(whole):
        i = count[0]
        count[0] += 1
        copy = pltpu.make_async_remote_copy(
            src_ref=whole, dst_ref=whole, send_sem=ss.at[i], recv_sem=rs.at[i], device_id=dev(dy=1), device_id_type=MESH
        )
        sent.append(copy)
        return i, copy

    ZORDER = [6, 5, 7, 4, 8, 3, 9, 2, 10, 1, 11]
    KORDER = [4, 3, -3, 2, -2, 1, -1, 0]

    def partial(st, c):
        rows = pl.ds(c * ROWS, ROWS)
        cols = pl.ds(st * HALF, HALF)
        for at, val in (
            (0, lambda: contract(tok[rows, :], wg[:, cols], (1, 0))),
            (1, lambda: contract(tok[rows, :], wu[:, cols], (1, 0))),
            (2, lambda: contract(og[rows, :], wd[:, cols], (1, 0))),
        ):
            part[st, c, :, :, :, at * HALF : (at + 1) * HALF] = val().reshape(NY, 2, U, HALF)

    def chain(value, long, sb, rb, sf, rf):
        got = {}
        todo = {}
        for sg, d in ((1, 0), (-1, 1)):
            first = 1 if sg == long else 2
            todo[sg] = (d, first)
        for s in range(1, 5):
            for sg in (1, -1):
                d, first = todo[sg]
                if s < first:
                    continue
                owner = ymod(y + sg * (5 - s))
                if s > first:
                    got[sg].wait_recv()
                val = value(owner, sg * (5 - s))
                if s > first:
                    val = val + rb[d, s - 2].astype(F32)
                if s == 4:
                    sf[d] = val
                    got[sg] = send(sf.at[d], rf.at[d], dev(dy=sg))
                else:
                    sb[d, s - 1] = val.astype(BF)
                    got[sg] = send(sb.at[d, s - 1], rb.at[d, s - 1], dev(dy=sg))
            yield T_Y
        for sg in (1, -1):
            got[sg].wait_recv()
        return value(y, 0) + rf[0] + rf[1]

    def spread(slot, long, arrived):
        got = {}
        for s in range(1, 5):
            for sg in (1, -1):
                if s == 4 and sg != long:
                    continue
                if s > 1:
                    got[sg].wait_recv()
                    arrived(ymod(y - sg * (s - 1)))
                at = slot(ymod(y - sg * (s - 1)))
                got[sg] = send(at, at, dev(dy=sg))
            yield T_Y
        got[long].wait_recv()
        arrived(ymod(y - long * 4))
        got[-long].wait_recv()
        arrived(ymod(y + long * 3))

    def keep(at, sums):
        hidden, gate_back, up_back = gating(sums)
        at[:, :HALF] = hidden
        at[:, HALF : 2 * HALF] = gate_back
        at[:, 2 * HALF :] = up_back

    def stream0(c):
        long = 1 if c % 2 == 0 else -1

        def value(owner, _):
            return part[0, c, owner]

        total = yield from chain(value, long, sb1.at[c], rb1.at[c], sf1.at[c], rf1.at[c])
        tx[c] = total
        got = send(tx.at[c], xr.at[c], dev(dxh=1))
        yield T_X
        got.wait_recv()
        for h in range(2):
            keep(gat1.at[c, y, h], tx[c, h] + xr[c, h])
        yield from spread(lambda o: gat1.at[c, o], long, lambda o: None)

    def stream1_open(c, out, ks):
        for k in ks:
            off = KORDER[k]
            sx[c, k] = part[1, c, ymod(y + off), 1 - xh].astype(BF)
            out[off] = send(sx.at[c, k], rx.at[c, k], dev(dxh=1))

    def stream1(c, from_x):
        long = -1 if c % 2 == 0 else 1
        ready = set()

        def value(owner, off):
            off = 4 if off == -4 else off
            if off not in ready:
                from_x[off].wait_recv()
                ready.add(off)
            k = KORDER.index(off)
            return part[1, c, owner, xh] + rx[c, k].astype(F32)

        yield T_OPEN[c]
        total = yield from chain(value, long, sb2.at[c], rb2.at[c], sf2.at[c], rf2.at[c])
        keep(gat2.at[c, y, xh], total)
        i, back = group(gat2.at[c, :, 1 - xh])

        def arrived(o):
            send(gat2.at[c, o, xh], gat2.at[c, o, xh], dev(dxh=1), i)

        arrived(y)
        yield from spread(lambda o: gat2.at[c, o, xh], long, arrived)
        yield T_X
        back.wait_recv()

    grads = []

    def weight_grad(i):
        left, cols, out, to = (
            (tok_t, 1, gbuf, gg),
            (tok_t, 2, ubuf, ug),
            (og_t, 0, dbuf, dg),
        )[i]
        for st, g in ((0, gat1), (1, gat2)):
            right = g[:, :, :, :, cols * HALF : (cols + 1) * HALF].reshape(TOKENS, HALF)
            out[:, st * HALF : (st + 1) * HALF] = contract(left[...], right, (1, 0))
        copy = pltpu.make_async_copy(out, to, ls.at[i])
        copy.start()
        local.append(copy)

    local = []

    def weight_grads():
        for i in range(3):
            weight_grad(i)
            yield 3.0

    def flush(c):
        if c == NC - 1:
            while len(sent) > 20:
                sent.pop(0).wait_send()

    def reduce(c):
        def side(weights, at):
            total = None
            for st, g in ((0, gat1), (1, gat2)):
                left = weights[:, st * HALF : (st + 1) * HALF]
                right = g[c, :, :, :, at * HALF : (at + 1) * HALF].reshape(ROWS, HALF)
                one = contract(left, right, (1, 1))
                total = one if total is None else total + one
            return total

        def put(m, val):
            for h in range(2):
                wp[c, m, h] = val[:, h * Q : (h + 1) * Q]

        put(0, side(wd, 0))
        put(1, side(wg, 1) + side(wu, 2))
        got = send(wp.at[c, 1 - co], cr.at[c], dev(dco=1))
        yield T_CORE
        got.wait_recv()
        av[c] = (wp[c, co, 1 - xl] + cr[c, 1 - xl]).astype(BF)
        got = send(av.at[c], xlr.at[c], dev(dxl=1))
        own = wp[c, co, xl] + cr[c, xl]
        wp[c, co, xl] = own
        yield T_XL
        got.wait_recv()
        own = (wp[c, co, xl] + xlr[c].astype(F32)).reshape(NZ, DM // NZ, Q)
        bv[c] = own
        bs[c, :, : DM // NZ] = own.astype(BF)
        i, got = group(zr.at[c])
        for d in ZORDER:
            send(bs.at[c, lax.rem(z + d, NZ)], zr.at[c, d - 1], dev(dz=d), i)
        flush(c)
        yield T_Z
        total = bv[c, z]
        got.wait_recv()
        for d in range(1, NZ):
            total = total + zr[c, d - 1, : DM // NZ].astype(F32)
        fin[c, co, xl, z, : DM // NZ] = total.astype(BF)
        mine = fin.at[c, co, xl, z]
        i, got = group(fin.at[c, co, xl, : NZ - 1])
        for d in ZORDER:
            send(mine, mine, dev(dz=d), i)
        flush(c)
        yield T_Z
        got.wait_recv()
        mine = fin.at[c, co, xl]
        across = send(mine, mine, dev(dxl=1))
        near = send(mine, mine, dev(dco=1))
        flush(c)
        yield T_XL
        across.wait_recv()
        mine = fin.at[c, co, 1 - xl]
        far = send(mine, mine, dev(dco=1))
        yield T_CORE
        near.wait_recv()
        far.wait_recv()
        for m, out in ((0, mixed), (1, tgrad)):
            for h in range(2):
                block = fin[c, m, h, :, : DM // NZ].reshape(DM, Q)
                out[:, c * ROWS + h * Q : c * ROWS + (h + 1) * Q] = block

    queue = []
    left = {c: 2 for c in range(NC)}

    def push(t, task, c, part):
        heapq.heappush(queue, (t, len(order), task, c, part))
        order.append(part)

    order = []
    opened = [{} for _ in range(NC)]

    def opening(c, at):
        if c == 0:
            loads["tok"].wait()
            tok[...] = tok_t[...].T
            loads["wg"].wait()
            loads["wu"].wait()
            loads["og"].wait()
            loads["wd"].wait()
            og[...] = og_t[...].T
        partial(0, c)
        if c == 0:
            pl.semaphore_wait(barrier, len(peers))
        push(at, stream0(c), c, True)
        yield 0.5
        partial(1, c)
        stream1_open(c, opened[c], range(5))
        push(at + 0.5, stream1(c, opened[c]), c, True)
        if c == NC - 1:
            for other in range(NC):
                stream1_open(other, opened[other], range(5, NY))
            fin[...] = jnp.zeros_like(fin)
            bs[...] = jnp.zeros_like(bs)

    for c in range(NC):
        push(c * LAG, opening(c, c * LAG), c, False)
    while queue:
        t, _, task, c, part_of = heapq.heappop(queue)
        try:
            push(t + next(task), task, c, part_of)
        except StopIteration:
            if part_of:
                left[c] -= 1
                if left[c] == 0:
                    push(t, reduce(c), c, False)
                    if not any(left.values()):
                        push(t + 0.1, weight_grads(), NC, False)
    for copy in sent:
        copy.wait_send()
    for copy in local:
        copy.wait()


def hand_over(*refs):
    held, sems = refs[10:15], refs[15]
    into = [pltpu.make_async_copy(refs[i], held[i], sems.at[0, i]) for i in range(5)]
    out = [pltpu.make_async_copy(held[i], refs[5 + i], sems.at[1, i]) for i in range(5)]
    for copy in into:
        copy.start()
    for first, second in zip(into, out):
        first.wait()
        second.start()
    for copy in out:
        copy.wait()


def shards(tokens, gate_weight, up_weight, down_weight, out_grad):
    vm = pl.BlockSpec(memory_space=pltpu.VMEM)
    hbm = pl.BlockSpec(memory_space=pl.ANY)
    V = pltpu.VMEM
    outs = pl.pallas_call(
        kernel,
        out_shape=(
            jax.ShapeDtypeStruct((DM, TOKENS), BF),
            jax.ShapeDtypeStruct((DM, TOKENS), BF),
            jax.ShapeDtypeStruct((DM, FF), F32),
            jax.ShapeDtypeStruct((DM, FF), F32),
            jax.ShapeDtypeStruct((DM, FF), F32),
        ),
        in_specs=[hbm] * 5,
        out_specs=(vm, vm, hbm, hbm, hbm),
        scratch_shapes=[
            V((2, NC, NY, 2, U, W3), F32),
            V((NC, 2, 3, 2, U, W3), BF),
            V((NC, 2, 3, 2, U, W3), BF),
            V((NC, 2, 2, U, W3), F32),
            V((NC, 2, 2, U, W3), F32),
            V((NC, 2, U, W3), F32),
            V((NC, 2, U, W3), F32),
            V((NC, NY, U, W3), BF),
            V((NC, NY, U, W3), BF),
            V((NC, 2, 3, U, W3), BF),
            V((NC, 2, 3, U, W3), BF),
            V((NC, 2, U, W3), F32),
            V((NC, 2, U, W3), F32),
            V((NC, NY, 2, U, W3), BF),
            V((NC, NY, 2, U, W3), BF),
            V((NC, 2, 2, DM, Q), F32),
            V((NC, 2, DM, Q), F32),
            V((NC, DM, Q), BF),
            V((NC, DM, Q), BF),
            V((NC, NZ, DM // NZ, Q), F32),
            V((NC, NZ, 32, Q), BF),
            V((NC, NZ - 1, 32, Q), BF),
            V((NC, 2, 2, NZ, 32, Q), BF),
            V((DM, FF), F32),
            V((DM, FF), F32),
            V((DM, FF), F32),
            V((TOKENS, DM), BF),
            V((TOKENS, DM), BF),
            V((DM, TOKENS), BF),
            V((DM, TOKENS), BF),
            V((DM, FF), BF),
            V((DM, FF), BF),
            V((DM, FF), BF),
            pltpu.SemaphoreType.DMA((NSEM,)),
            pltpu.SemaphoreType.DMA((NSEM,)),
            pltpu.SemaphoreType.DMA((3,)),
            pltpu.SemaphoreType.DMA((5,)),
        ],
        compiler_params=pltpu.CompilerParams(
            collective_id=0, has_side_effects=True, vmem_limit_bytes=56 << 20
        ),
        name="swiglu",
    )(tokens.T, out_grad.T, gate_weight, up_weight, down_weight.T)
    outs = pl.pallas_call(
        hand_over,
        out_shape=tuple(jax.ShapeDtypeStruct(o.shape, o.dtype) for o in outs),
        in_specs=[hbm] * 5,
        out_specs=(hbm,) * 5,
        scratch_shapes=[V(o.shape, o.dtype) for o in outs] + [pltpu.SemaphoreType.DMA((2, 5))],
        name="hand_over",
    )(*outs)
    mixed, tgrad, gg, ug, dg = outs
    return mixed.T, tgrad.T, gg, ug, dg.T


def solution(mesh):
    placed = (P(None, "tp"), P("tp", "fsdp"), P("tp", "fsdp"), P("fsdp", "tp"), P(None, "tp"))
    return jax.shard_map(
        shards,
        mesh=mesh,
        in_specs=placed,
        out_specs=(P(None, "tp"), P(None, "tp"), P("tp", "fsdp"), P("tp", "fsdp"), P("fsdp", "tp")),
        check_vma=False,
    )
```

```python
import heapq

import jax
import jax.numpy as jnp
from jax import lax
from jax.experimental import pallas as pl
from jax.experimental.pallas import tpu as pltpu
from jax.sharding import PartitionSpec as P

MESH = pl.DeviceIdType.MESH
BF, F32 = jnp.bfloat16, jnp.float32
NY, NZ = 8, 12
TOKENS, DM, FF = 512, 288, 768
NC = 2
ROWS = TOKENS // NC
U = ROWS // 16
HID = (FF // 3, FF - FF // 3)
AT = (0, HID[0])
WIDE = tuple(3 * h for h in HID)
Q = ROWS // 2
NSEM = 45 * NC
NOWN, OWN = 9, 32
ZT = BF
LAG, T_Y, T_X, T_CORE, T_XL, T_Z = 1.5, 4.0, 4.5, 2.5, 3.6, 5.0
T_OPEN = (3.5, 5.0)


def contract(left, right, dims):
    return lax.dot_general(left, right, ((dims[:1], dims[1:]), ((), ())), preferred_element_type=F32)


def gating(sums, n):
    gate, up, back = sums[:, :n], sums[:, n : 2 * n], sums[:, 2 * n :]
    sig = jax.nn.sigmoid(gate)
    activated = gate * sig
    hidden = (activated * up).astype(BF)
    up_back = (back * activated).astype(BF)
    gate_back = (back * up * sig * (1.0 + gate * (1.0 - sig))).astype(BF)
    return hidden, gate_back, up_back


def kernel(
    tok_h, og_h, wg_h, wu_h, wd_h,
    mixed, tgrad, gg, ug, dg,
    part1, part2, sb1, rb1, sf1, rf1, tx, xr, sx, rx, sb2, rb2, sf2, rf2, gat1, gat2,
    wp, cr, av, xlr, bv, zr, fin, zall, tok, og, tok_t, og_t, wg, wu, wd,
    ss, rs, ins,
):
    tp, fs = lax.axis_index("tp"), lax.axis_index("fsdp")
    y, xh = tp // 2, tp % 2
    xl, z, co = fs // 24, (fs // 2) % NZ, fs % 2

    def ymod(v):
        return lax.rem(v + 2 * NY, NY)

    def dev(dy=0, dxh=0, dxl=0, dz=0, dco=0):
        ny = ymod(y + dy)
        nxh = 1 - xh if dxh else xh
        nxl = 1 - xl if dxl else xl
        nz = lax.rem(z + dz, NZ)
        nco = 1 - co if dco else co
        return (ny * 2 + nxh, (nxl * NZ + nz) * 2 + nco)

    barrier = pltpu.get_barrier_semaphore()
    peers = [dev(dy=1), dev(dy=-1), dev(dxh=1), dev(dxl=1), dev(dco=1)]
    peers += [dev(dz=d) for d in range(1, NZ)]
    for peer in peers:
        pl.semaphore_signal(barrier, inc=1, device_id=peer, device_id_type=MESH)

    loads = {}
    for i, (name, a, b) in enumerate(
        (("tok", tok_h, tok_t), ("wg", wg_h, wg), ("wu", wu_h, wu), ("og", og_h, og_t), ("wd", wd_h, wd))
    ):
        loads[name] = pltpu.make_async_copy(a, b, ins.at[i])
        loads[name].start()

    sent = []
    count = [0]

    def send(src, dst, to, at=None):
        i = count[0] if at is None else at
        count[0] += at is None
        copy = pltpu.make_async_remote_copy(
            src_ref=src, dst_ref=dst, send_sem=ss.at[i], recv_sem=rs.at[i], device_id=to, device_id_type=MESH
        )
        copy.start()
        if at is None:
            sent.append(copy)
        return copy

    def alone():
        count[0] += 1
        return count[0] - 1

    def tally(whole, i):
        return pltpu.make_async_remote_copy(
            src_ref=whole, dst_ref=whole, send_sem=ss.at[i], recv_sem=rs.at[i], device_id=dev(dy=1), device_id_type=MESH
        )

    def group(whole):
        i = alone()
        copy = tally(whole, i)
        sent.append(copy)
        return i, copy

    ZORDER = [6, 5, 7, 4, 8, 3, 9, 2, 10, 1, 11]
    KORDER = [4, 3, -3, 2, -2, 1, -1, 0]

    parts = (part1, part2)

    def partial(st, c):
        rows = pl.ds(c * ROWS, ROWS)
        n = HID[st]
        cols = pl.ds(AT[st], n)
        for at, val in (
            (0, lambda: contract(tok[rows, :], wg[:, cols], (1, 0))),
            (1, lambda: contract(tok[rows, :], wu[:, cols], (1, 0))),
            (2, lambda: contract(og[rows, :], wd[:, cols], (1, 0))),
        ):
            parts[st][c, :, :, :, at * n : (at + 1) * n] = val().reshape(NY, 2, U, n)

    def chain(value, long, sb, rb, sf, rf):
        got = {}
        todo = {}
        for sg, d in ((1, 0), (-1, 1)):
            first = 1 if sg == long else 2
            todo[sg] = (d, first)
        for s in range(1, 5):
            for sg in (1, -1):
                d, first = todo[sg]
                if s < first:
                    continue
                owner = ymod(y + sg * (5 - s))
                if s > first:
                    got[sg].wait_recv()
                val = value(owner, sg * (5 - s))
                if s > first:
                    val = val + rb[d, s - 2].astype(F32)
                if s == 4:
                    sf[d] = val
                    got[sg] = send(sf.at[d], rf.at[d], dev(dy=sg))
                else:
                    sb[d, s - 1] = val.astype(BF)
                    got[sg] = send(sb.at[d, s - 1], rb.at[d, s - 1], dev(dy=sg))
            yield T_Y
        for sg in (1, -1):
            got[sg].wait_recv()
        return value(y, 0) + rf[0] + rf[1]

    def spread(slot, long, arrived):
        got = {}
        for s in range(1, 5):
            for sg in (1, -1):
                if s == 4 and sg != long:
                    continue
                if s > 1:
                    got[sg].wait_recv()
                at = slot(ymod(y - sg * (s - 1)))
                got[sg] = send(at, at, dev(dy=sg))
                if s > 1:
                    arrived(ymod(y - sg * (s - 1)))
            yield T_Y
        got[long].wait_recv()
        arrived(ymod(y - long * 4))
        got[-long].wait_recv()
        arrived(ymod(y + long * 3))

    def keep(at, sums):
        n = sums.shape[1] // 3
        hidden, gate_back, up_back = gating(sums, n)
        at[:, :n] = hidden
        at[:, n : 2 * n] = gate_back
        at[:, 2 * n :] = up_back

    def stream0(c):
        long = 1 if c % 2 == 0 else -1

        def value(owner, _):
            return part1[c, owner]

        total = yield from chain(value, long, sb1.at[c], rb1.at[c], sf1.at[c], rf1.at[c])
        tx[c] = total
        got = send(tx.at[c], xr.at[c], dev(dxh=1))
        yield T_X
        got.wait_recv()
        for h in range(2):
            keep(gat1.at[c, y, h], tx[c, h] + xr[c, h])
        yield from spread(lambda o: gat1.at[c, o], long, lambda o: None)

    def stream1_open(c, out, ks):
        for k in ks:
            off = KORDER[k]
            sx[c, k] = part2[c, ymod(y + off), 1 - xh].astype(BF)
            out[off] = send(sx.at[c, k], rx.at[c, k], dev(dxh=1))

    def stream1(c, from_x):
        long = -1 if c % 2 == 0 else 1
        ready = set()

        def value(owner, off):
            off = 4 if off == -4 else off
            if off not in ready:
                from_x[off].wait_recv()
                ready.add(off)
            k = KORDER.index(off)
            return part2[c, owner, xh] + rx[c, k].astype(F32)

        yield T_OPEN[c]
        total = yield from chain(value, long, sb2.at[c], rb2.at[c], sf2.at[c], rf2.at[c])
        keep(gat2.at[c, y, xh], total)
        i, back = group(gat2.at[c, :, 1 - xh])

        def arrived(o):
            send(gat2.at[c, o, xh], gat2.at[c, o, xh], dev(dxh=1), i)

        arrived(y)
        yield from spread(lambda o: gat2.at[c, o, xh], long, arrived)
        yield T_X
        back.wait_recv()

    grads = []

    def weight_grad(i):
        left, cols, out = (
            (tok_t, 1, gg),
            (tok_t, 2, ug),
            (og_t, 0, dg),
        )[i]
        for st, g in ((0, gat1), (1, gat2)):
            n = HID[st]
            right = g[:, :, :, :, cols * n : (cols + 1) * n].reshape(TOKENS, n)
            out[:, AT[st] : AT[st] + n] = contract(left[...], right, (1, 0))

    def weight_grads():
        for i in range(3):
            weight_grad(i)
            yield 3.0

    def flush(c):
        if c == NC - 1:
            while len(sent) > 20:
                sent.pop(0).wait_send()

    def reduce(c):
        def side(weights, at):
            total = None
            for st, g in ((0, gat1), (1, gat2)):
                n = HID[st]
                left = weights[:, AT[st] : AT[st] + n]
                right = g[c, :, :, :, at * n : (at + 1) * n].reshape(ROWS, n)
                one = contract(left, right, (1, 1))
                total = one if total is None else total + one
            return total

        def put(m, val):
            for h in range(2):
                wp[c, m, h] = val[:, h * Q : (h + 1) * Q]

        put(0, side(wd, 0))
        put(1, side(wg, 1) + side(wu, 2))
        got = send(wp.at[c, 1 - co], cr.at[c], dev(dco=1))
        yield T_CORE
        got.wait_recv()
        av[c] = (wp[c, co, 1 - xl] + cr[c, 1 - xl]).astype(BF)
        got = send(av.at[c], xlr.at[c], dev(dxl=1))
        own = wp[c, co, xl] + cr[c, xl]
        wp[c, co, xl] = own
        yield T_XL
        got.wait_recv()
        own = (wp[c, co, xl] + xlr[c].astype(F32)).reshape(NOWN, OWN, Q)
        bv[c] = own.astype(ZT)
        i = alone()
        for d in ZORDER:
            zt = lax.rem(z + d, NZ)

            @pl.when(zt % 4 != 3)
            def _(d=d, zt=zt):
                send(bv.at[c, zt - zt // 4], zr.at[c, d - 1], dev(dz=d), i)

        k = alone()
        mine = fin.at[c, co, xl, z - z // 4]
        flush(c)
        yield T_Z

        @pl.when(z % 4 != 3)
        def _():
            tally(zr.at[c], i).wait_recv()
            total = bv[c, z - z // 4].astype(F32)
            for d in range(1, NZ):
                total = total + zr[c, d - 1].astype(F32)
            fin[c, co, xl, z - z // 4] = total.astype(BF)
            for d in ZORDER:
                send(mine, mine, dev(dz=d), k)

        flush(c)
        yield T_Z

        @pl.when(z % 4 != 3)
        def _():
            tally(fin.at[c, co, xl, : NOWN - 1], k).wait_recv()
            tally(bv.at[c, : NOWN - 1], i).wait_send()
            tally(zall.at[c], k).wait_send()

        @pl.when(z % 4 == 3)
        def _():
            tally(fin.at[c, co, xl], k).wait_recv()
            tally(bv.at[c], i).wait_send()

        mine = fin.at[c, co, xl]
        across = send(mine, mine, dev(dxl=1))
        near = send(mine, mine, dev(dco=1))
        flush(c)
        yield T_XL
        across.wait_recv()
        mine = fin.at[c, co, 1 - xl]
        far = send(mine, mine, dev(dco=1))
        yield T_CORE
        near.wait_recv()
        far.wait_recv()
        for m, out in ((0, mixed), (1, tgrad)):
            for h in range(2):
                block = fin[c, m, h].reshape(DM, Q)
                out[:, c * ROWS + h * Q : c * ROWS + (h + 1) * Q] = block

    queue = []
    left = {c: 2 for c in range(NC)}

    def push(t, task, c, part):
        heapq.heappush(queue, (t, len(order), task, c, part))
        order.append(part)

    order = []
    opened = [{} for _ in range(NC)]

    def opening(c, at):
        if c == 0:
            loads["tok"].wait()
            tok[...] = tok_t[...].T
            loads["wg"].wait()
            loads["wu"].wait()
            loads["og"].wait()
            loads["wd"].wait()
            og[...] = og_t[...].T
        partial(0, c)
        if c == 0:
            pl.semaphore_wait(barrier, len(peers))
        push(at, stream0(c), c, True)
        yield 0.5
        partial(1, c)
        stream1_open(c, opened[c], range(5))
        push(at + 0.5, stream1(c, opened[c]), c, True)
        if c == NC - 1:
            for other in range(NC):
                stream1_open(other, opened[other], range(5, NY))

    for c in range(NC):
        push(c * LAG, opening(c, c * LAG), c, False)
    while queue:
        t, _, task, c, part_of = heapq.heappop(queue)
        try:
            push(t + next(task), task, c, part_of)
        except StopIteration:
            if part_of:
                left[c] -= 1
                if left[c] == 0:
                    push(t, reduce(c), c, False)
                    if not any(left.values()):
                        push(t + 0.1, weight_grads(), NC, False)
    for copy in sent:
        copy.wait_send()


def hand_over(*refs):
    copies = [pltpu.make_async_copy(refs[i], refs[5 + i], refs[10].at[i]) for i in range(5)]
    for copy in copies:
        copy.start()
    for copy in copies:
        copy.wait()


def shards(tokens, gate_weight, up_weight, down_weight, out_grad):
    vm = pl.BlockSpec(memory_space=pltpu.VMEM)
    hbm = pl.BlockSpec(memory_space=pl.ANY)
    V = pltpu.VMEM
    outs = pl.pallas_call(
        kernel,
        out_shape=(
            V((DM, TOKENS), BF),
            V((DM, TOKENS), BF),
            V((DM, FF), F32),
            V((DM, FF), F32),
            V((DM, FF), F32),
        ),
        in_specs=[hbm] * 5,
        out_specs=(vm,) * 5,
        scratch_shapes=[
            V((NC, NY, 2, U, WIDE[0]), F32),
            V((NC, NY, 2, U, WIDE[1]), F32),
            V((NC, 2, 3, 2, U, WIDE[0]), BF),
            V((NC, 2, 3, 2, U, WIDE[0]), BF),
            V((NC, 2, 2, U, WIDE[0]), F32),
            V((NC, 2, 2, U, WIDE[0]), F32),
            V((NC, 2, U, WIDE[0]), F32),
            V((NC, 2, U, WIDE[0]), F32),
            V((NC, NY, U, WIDE[1]), BF),
            V((NC, NY, U, WIDE[1]), BF),
            V((NC, 2, 3, U, WIDE[1]), BF),
            V((NC, 2, 3, U, WIDE[1]), BF),
            V((NC, 2, U, WIDE[1]), F32),
            V((NC, 2, U, WIDE[1]), F32),
            V((NC, NY, 2, U, WIDE[0]), BF),
            V((NC, NY, 2, U, WIDE[1]), BF),
            V((NC, 2, 2, DM, Q), F32),
            V((NC, 2, DM, Q), F32),
            V((NC, DM, Q), BF),
            V((NC, DM, Q), BF),
            V((NC, NOWN, OWN, Q), ZT),
            V((NC, NZ - 1, OWN, Q), ZT),
            V((NC, 2, 2, NOWN, OWN, Q), BF),
            V((NC, NZ - 1, OWN, Q), BF),
            V((TOKENS, DM), BF),
            V((TOKENS, DM), BF),
            V((DM, TOKENS), BF),
            V((DM, TOKENS), BF),
            V((DM, FF), BF),
            V((DM, FF), BF),
            V((DM, FF), BF),
            pltpu.SemaphoreType.DMA((NSEM,)),
            pltpu.SemaphoreType.DMA((NSEM,)),
            pltpu.SemaphoreType.DMA((5,)),
        ],
        compiler_params=pltpu.CompilerParams(
            collective_id=0, has_side_effects=True, vmem_limit_bytes=56 << 20
        ),
        name="swiglu",
    )(tokens.T, out_grad.T, gate_weight, up_weight, down_weight.T)
    outs = [pltpu.with_memory_space_constraint(o, pltpu.VMEM) for o in outs]
    outs = pl.pallas_call(
        hand_over,
        out_shape=tuple(jax.ShapeDtypeStruct(o.shape, o.dtype) for o in outs),
        in_specs=[hbm] * 5,
        out_specs=(hbm,) * 5,
        scratch_shapes=[pltpu.SemaphoreType.DMA((5,))],
        name="hand_over",
    )(*outs)
    mixed, tgrad, gg, ug, dg = outs
    return mixed.T, tgrad.T, gg, ug, dg.T


def solution(mesh):
    placed = (P(None, "tp"), P("tp", "fsdp"), P("tp", "fsdp"), P("fsdp", "tp"), P(None, "tp"))
    return jax.shard_map(
        shards,
        mesh=mesh,
        in_specs=placed,
        out_specs=(P(None, "tp"), P(None, "tp"), P("tp", "fsdp"), P("tp", "fsdp"), P("fsdp", "tp")),
        check_vma=False,
    )
```

```python
import heapq

import jax
import jax.numpy as jnp
from jax import lax
from jax.experimental import pallas as pl
from jax.experimental.pallas import tpu as pltpu
from jax.sharding import PartitionSpec as P

MESH = pl.DeviceIdType.MESH
BF, F32 = jnp.bfloat16, jnp.float32
NY, NZ = 8, 12
TOKENS, DM, FF = 512, 288, 768
NC = 2
ROWS = TOKENS // NC
U = ROWS // 16
HID = (FF // 3, FF - FF // 3)
AT = (0, HID[0])
WIDE = tuple(3 * h for h in HID)
Q = ROWS // 2
NSEND, NRECV = 16 * NC, 45 * NC
NOWN, OWN = 9, 32
LAG, T_Y, T_X, T_CORE, T_XL, T_Z = 1.5, 4.0, 4.5, 2.5, 3.6, 5.0
T_OPEN = (3.5, 5.0)


def contract(left, right, dims):
    return lax.dot_general(left, right, ((dims[:1], dims[1:]), ((), ())), preferred_element_type=F32)


def gating(sums, n):
    gate, up, back = sums[:, :n], sums[:, n : 2 * n], sums[:, 2 * n :]
    sig = jax.nn.sigmoid(gate)
    activated = gate * sig
    hidden = (activated * up).astype(BF)
    up_back = (back * activated).astype(BF)
    gate_back = (back * up * sig * (1.0 + gate * (1.0 - sig))).astype(BF)
    return hidden, gate_back, up_back


def kernel(
    tok_h, og_h, wg_h, wu_h, wd_h,
    mixed, tgrad, gg, ug, dg,
    part1, part2, sb1, rb1, sf1, rf1, tx, xr, sx, rx, sb2, rb2, sf2, rf2, gat1, gat2,
    wp, cr, av, xlr, bv, bw, zr, fin, zall, tok, og, tok_t, og_t, wg, wu, wd,
    ss, rs, ins,
):
    tp, fs = lax.axis_index("tp"), lax.axis_index("fsdp")
    y, xh = tp // 2, tp % 2
    xl, z, co = fs // 24, (fs // 2) % NZ, fs % 2

    def ymod(v):
        return lax.rem(v + 2 * NY, NY)

    def dev(dy=0, dxh=0, dxl=0, dz=0, dco=0):
        ny = ymod(y + dy)
        nxh = 1 - xh if dxh else xh
        nxl = 1 - xl if dxl else xl
        nz = lax.rem(z + dz, NZ)
        nco = 1 - co if dco else co
        return (ny * 2 + nxh, (nxl * NZ + nz) * 2 + nco)

    barrier = pltpu.get_barrier_semaphore()
    peers = [dev(dy=1), dev(dy=-1), dev(dxh=1), dev(dxl=1), dev(dco=1)]
    peers += [dev(dz=d) for d in range(1, NZ)]
    for peer in peers:
        pl.semaphore_signal(barrier, inc=1, device_id=peer, device_id_type=MESH)

    loads = {}
    for i, (name, a, b) in enumerate(
        (("tok", tok_h, tok_t), ("wg", wg_h, wg), ("wu", wu_h, wu), ("og", og_h, og_t), ("wd", wd_h, wd))
    ):
        loads[name] = pltpu.make_async_copy(a, b, ins.at[i])
        loads[name].start()

    sent = []
    used = [0, 0]

    def fresh(side):
        used[side] += 1
        return used[side] - 1

    def send(src, dst, to, at=None, out=None):
        if at is not None:
            o, i = at
        else:
            o, i = fresh(0) if out is None else out, fresh(1)
        copy = pltpu.make_async_remote_copy(
            src_ref=src, dst_ref=dst, send_sem=ss.at[o], recv_sem=rs.at[i], device_id=to, device_id_type=MESH
        )
        copy.start()
        if at is None and out is None:
            sent.append(copy)
        return copy

    def alone():
        return fresh(0), fresh(1)

    def tally(whole, at):
        return pltpu.make_async_remote_copy(
            src_ref=whole, dst_ref=whole, send_sem=ss.at[at[0]], recv_sem=rs.at[at[1]], device_id=dev(dy=1), device_id_type=MESH
        )

    def group(whole):
        at = alone()
        copy = tally(whole, at)
        sent.append(copy)
        return at, copy

    ZORDER = [6, 5, 7, 4, 8, 3, 9, 2, 10, 1, 11]
    KORDER = [4, 3, -3, 2, -2, 1, -1, 0]

    parts = (part1, part2)

    def partial(st, c):
        rows = pl.ds(c * ROWS, ROWS)
        n = HID[st]
        cols = pl.ds(AT[st], n)
        for at, val in (
            (0, lambda: contract(tok[rows, :], wg[:, cols], (1, 0))),
            (1, lambda: contract(tok[rows, :], wu[:, cols], (1, 0))),
            (2, lambda: contract(og[rows, :], wd[:, cols], (1, 0))),
        ):
            parts[st][c, :, :, :, at * n : (at + 1) * n] = val().reshape(NY, 2, U, n)

    def chain(value, long, sb, rb, sf, rf, five):
        got = {}
        narrow, wide = fresh(0), fresh(0)
        todo = {}
        for sg, d in ((1, 0), (-1, 1)):
            first = 1 if sg == long else 2
            todo[sg] = (d, first)
        for s in range(1, 5):
            for sg in (1, -1):
                d, first = todo[sg]
                if s < first:
                    continue
                owner = ymod(y + sg * (5 - s))
                if s > first:
                    got[sg].wait_recv()
                val = value(owner, sg * (5 - s))
                if s > first:
                    val = val + rb[d, s - 2].astype(F32)
                if s == 4:
                    sf[d] = val
                    got[sg] = send(sf.at[d], rf.at[d], dev(dy=sg), out=wide)
                else:
                    sb[d, s - 1] = val.astype(BF)
                    got[sg] = send(sb.at[d, s - 1], rb.at[d, s - 1], dev(dy=sg), out=narrow)
            yield T_Y
        for sg in (1, -1):
            got[sg].wait_recv()
        sent.extend((tally(five, (narrow, 0)), tally(sf, (wide, 0))))
        return value(y, 0) + rf[0] + rf[1]

    def spread(slot, long, arrived, seven):
        got = {}
        out = fresh(0)
        for s in range(1, 5):
            for sg in (1, -1):
                if s == 4 and sg != long:
                    continue
                if s > 1:
                    got[sg].wait_recv()
                at = slot(ymod(y - sg * (s - 1)))
                got[sg] = send(at, at, dev(dy=sg), out=out)
                if s > 1:
                    arrived(ymod(y - sg * (s - 1)))
            yield T_Y
        got[long].wait_recv()
        arrived(ymod(y - long * 4))
        got[-long].wait_recv()
        arrived(ymod(y + long * 3))
        sent.append(tally(seven, (out, 0)))

    def keep(at, sums):
        n = sums.shape[1] // 3
        hidden, gate_back, up_back = gating(sums, n)
        at[:, :n] = hidden
        at[:, n : 2 * n] = gate_back
        at[:, 2 * n :] = up_back

    def stream0(c):
        long = 1 if c % 2 == 0 else -1

        def value(owner, _):
            return part1[c, owner]

        total = yield from chain(value, long, sb1.at[c], rb1.at[c], sf1.at[c], rf1.at[c], gat1.at[c, :5])
        tx[c] = total
        got = send(tx.at[c], xr.at[c], dev(dxh=1))
        yield T_X
        got.wait_recv()
        for h in range(2):
            keep(gat1.at[c, y, h], tx[c, h] + xr[c, h])
        yield from spread(lambda o: gat1.at[c, o], long, lambda o: None, gat1.at[c, :7])

    xsem = {}

    def stream1_open(c, out, ks):
        for k in ks:
            off = KORDER[k]
            sx[c, k] = part2[c, ymod(y + off), 1 - xh].astype(BF)
            if not out:
                xsem[c] = fresh(0)
            out[off] = send(sx.at[c, k], rx.at[c, k], dev(dxh=1), out=xsem[c])
            if k == NY - 1:
                sent.append(tally(sx.at[c], (xsem[c], 0)))

    def stream1(c, from_x):
        long = -1 if c % 2 == 0 else 1
        ready = set()

        def value(owner, off):
            off = 4 if off == -4 else off
            if off not in ready:
                from_x[off].wait_recv()
                ready.add(off)
            k = KORDER.index(off)
            return part2[c, owner, xh] + rx[c, k].astype(F32)

        yield T_OPEN[c]
        total = yield from chain(value, long, sb2.at[c], rb2.at[c], sf2.at[c], rf2.at[c], sx.at[c, :5])
        keep(gat2.at[c, y, xh], total)
        i, back = group(gat2.at[c, :, 1 - xh])

        def arrived(o):
            send(gat2.at[c, o, xh], gat2.at[c, o, xh], dev(dxh=1), i)

        arrived(y)
        yield from spread(lambda o: gat2.at[c, o, xh], long, arrived, sx.at[c, :7])
        yield T_X
        back.wait_recv()

    grads = []

    def weight_grad(i):
        left, cols, out = (
            (tok_t, 1, gg),
            (tok_t, 2, ug),
            (og_t, 0, dg),
        )[i]
        for st, g in ((0, gat1), (1, gat2)):
            n = HID[st]
            right = g[:, :, :, :, cols * n : (cols + 1) * n].reshape(TOKENS, n)
            out[:, AT[st] : AT[st] + n] = contract(left[...], right, (1, 0))

    def weight_grads():
        for i in range(3):
            weight_grad(i)
            yield 3.0

    def flush(c):
        if c == NC - 1:
            while len(sent) > 8:
                sent.pop(0).wait_send()

    def reduce(c):
        def side(weights, at):
            total = None
            for st, g in ((0, gat1), (1, gat2)):
                n = HID[st]
                left = weights[:, AT[st] : AT[st] + n]
                right = g[c, :, :, :, at * n : (at + 1) * n].reshape(ROWS, n)
                one = contract(left, right, (1, 1))
                total = one if total is None else total + one
            return total

        def put(m, val):
            for h in range(2):
                wp[c, m, h] = val[:, h * Q : (h + 1) * Q]

        put(0, side(wd, 0))
        put(1, side(wg, 1) + side(wu, 2))
        got = send(wp.at[c, 1 - co], cr.at[c], dev(dco=1))
        yield T_CORE
        got.wait_recv()
        av[c] = wp[c, co, 1 - xl] + cr[c, 1 - xl]
        got = send(av.at[c], xlr.at[c], dev(dxl=1))
        own = wp[c, co, xl] + cr[c, xl]
        wp[c, co, xl] = own
        yield T_XL
        got.wait_recv()
        own = (wp[c, co, xl] + xlr[c]).reshape(NOWN, OWN, Q)
        bv[c] = own.astype(BF)
        bw[c] = own
        i = alone()
        for d in ZORDER:
            zt = lax.rem(z + d, NZ)

            @pl.when(zt % 4 != 3)
            def _(d=d, zt=zt):
                send(bv.at[c, zt - zt // 4], zr.at[c, d - 1], dev(dz=d), i)

        k = alone()
        mine = fin.at[c, co, xl, z - z // 4]
        flush(c)
        yield T_Z

        @pl.when(z % 4 != 3)
        def _():
            tally(zr.at[c], i).wait_recv()
            total = bw[c, z - z // 4]
            for d in range(1, NZ):
                total = total + zr[c, d - 1].astype(F32)
            fin[c, co, xl, z - z // 4] = total.astype(BF)
            for d in ZORDER:
                send(mine, mine, dev(dz=d), k)

        flush(c)
        yield T_Z

        @pl.when(z % 4 != 3)
        def _():
            tally(fin.at[c, co, xl, : NOWN - 1], k).wait_recv()
            tally(bv.at[c, : NOWN - 1], i).wait_send()
            tally(zall.at[c], k).wait_send()

        @pl.when(z % 4 == 3)
        def _():
            tally(fin.at[c, co, xl], k).wait_recv()
            tally(bv.at[c], i).wait_send()

        mine = fin.at[c, co, xl]
        across = send(mine, mine, dev(dxl=1))
        near = send(mine, mine, dev(dco=1))
        flush(c)
        yield T_XL
        across.wait_recv()
        mine = fin.at[c, co, 1 - xl]
        far = send(mine, mine, dev(dco=1))
        yield T_CORE
        near.wait_recv()
        far.wait_recv()
        for m, out in ((0, mixed), (1, tgrad)):
            for h in range(2):
                block = fin[c, m, h].reshape(DM, Q)
                out[:, c * ROWS + h * Q : c * ROWS + (h + 1) * Q] = block

    queue = []
    left = {c: 2 for c in range(NC)}

    def push(t, task, c, part):
        heapq.heappush(queue, (t, len(order), task, c, part))
        order.append(part)

    order = []
    opened = [{} for _ in range(NC)]

    def opening(c, at):
        if c == 0:
            loads["tok"].wait()
            tok[...] = tok_t[...].T
            loads["wg"].wait()
            loads["wu"].wait()
            loads["og"].wait()
            loads["wd"].wait()
            og[...] = og_t[...].T
        partial(0, c)
        if c == 0:
            pl.semaphore_wait(barrier, len(peers))
        push(at, stream0(c), c, True)
        yield 0.5
        partial(1, c)
        stream1_open(c, opened[c], range(5))
        push(at + 0.5, stream1(c, opened[c]), c, True)
        if c == NC - 1:
            for other in range(NC):
                stream1_open(other, opened[other], range(5, NY))

    for c in range(NC):
        push(c * LAG, opening(c, c * LAG), c, False)
    while queue:
        t, _, task, c, part_of = heapq.heappop(queue)
        try:
            push(t + next(task), task, c, part_of)
        except StopIteration:
            if part_of:
                left[c] -= 1
                if left[c] == 0:
                    push(t, reduce(c), c, False)
                    if not any(left.values()):
                        push(t + 0.1, weight_grads(), NC, False)
    for copy in sent:
        copy.wait_send()


def hand_over(*refs):
    copies = [pltpu.make_async_copy(refs[i], refs[5 + i], refs[10].at[i]) for i in range(5)]
    for copy in copies:
        copy.start()
    for copy in copies:
        copy.wait()


def shards(tokens, gate_weight, up_weight, down_weight, out_grad):
    vm = pl.BlockSpec(memory_space=pltpu.VMEM)
    hbm = pl.BlockSpec(memory_space=pl.ANY)
    V = pltpu.VMEM
    outs = pl.pallas_call(
        kernel,
        out_shape=(
            V((DM, TOKENS), BF),
            V((DM, TOKENS), BF),
            V((DM, FF), F32),
            V((DM, FF), F32),
            V((DM, FF), F32),
        ),
        in_specs=[hbm] * 5,
        out_specs=(vm,) * 5,
        scratch_shapes=[
            V((NC, NY, 2, U, WIDE[0]), F32),
            V((NC, NY, 2, U, WIDE[1]), F32),
            V((NC, 2, 3, 2, U, WIDE[0]), BF),
            V((NC, 2, 3, 2, U, WIDE[0]), BF),
            V((NC, 2, 2, U, WIDE[0]), F32),
            V((NC, 2, 2, U, WIDE[0]), F32),
            V((NC, 2, U, WIDE[0]), F32),
            V((NC, 2, U, WIDE[0]), F32),
            V((NC, NY, U, WIDE[1]), BF),
            V((NC, NY, U, WIDE[1]), BF),
            V((NC, 2, 3, U, WIDE[1]), BF),
            V((NC, 2, 3, U, WIDE[1]), BF),
            V((NC, 2, U, WIDE[1]), F32),
            V((NC, 2, U, WIDE[1]), F32),
            V((NC, NY, 2, U, WIDE[0]), BF),
            V((NC, NY, 2, U, WIDE[1]), BF),
            V((NC, 2, 2, DM, Q), F32),
            V((NC, 2, DM, Q), F32),
            V((NC, DM, Q), F32),
            V((NC, DM, Q), F32),
            V((NC, NOWN, OWN, Q), BF),
            V((NC, NOWN, OWN, Q), F32),
            V((NC, NZ - 1, OWN, Q), BF),
            V((NC, 2, 2, NOWN, OWN, Q), BF),
            V((NC, NZ - 1, OWN, Q), BF),
            V((TOKENS, DM), BF),
            V((TOKENS, DM), BF),
            V((DM, TOKENS), BF),
            V((DM, TOKENS), BF),
            V((DM, FF), BF),
            V((DM, FF), BF),
            V((DM, FF), BF),
            pltpu.SemaphoreType.DMA((NSEND,)),
            pltpu.SemaphoreType.DMA((NRECV,)),
            pltpu.SemaphoreType.DMA((5,)),
        ],
        compiler_params=pltpu.CompilerParams(
            collective_id=0, has_side_effects=True, vmem_limit_bytes=56 << 20
        ),
        name="swiglu",
    )(tokens.T, out_grad.T, gate_weight, up_weight, down_weight.T)
    outs = [pltpu.with_memory_space_constraint(o, pltpu.VMEM) for o in outs]
    outs = pl.pallas_call(
        hand_over,
        out_shape=tuple(jax.ShapeDtypeStruct(o.shape, o.dtype) for o in outs),
        in_specs=[hbm] * 5,
        out_specs=(hbm,) * 5,
        scratch_shapes=[pltpu.SemaphoreType.DMA((5,))],
        name="hand_over",
    )(*outs)
    mixed, tgrad, gg, ug, dg = outs
    return mixed.T, tgrad.T, gg, ug, dg.T


def solution(mesh):
    placed = (P(None, "tp"), P("tp", "fsdp"), P("tp", "fsdp"), P("fsdp", "tp"), P(None, "tp"))
    return jax.shard_map(
        shards,
        mesh=mesh,
        in_specs=placed,
        out_specs=(P(None, "tp"), P(None, "tp"), P("tp", "fsdp"), P("tp", "fsdp"), P("fsdp", "tp")),
        check_vma=False,
    )
```
